256 devices in a mesh: pair: 8 (over x, core), slab: 32 (over y, z).
Axes of the slice: x: 4, y: 4, z: 8, core: 2. Of those that a mesh axis runs over, the one named last changes fastest.
Arguments:
- amplitudes: bfloat16 [1024, 640, 640], P('pair', 'slab'), may hold values from -6 to 6
- integrals: bfloat16 [640, 640, 1024], P('slab', 'pair'), may hold values from -0.013671875 to 0.013671875
- block_map: int32 [10, 10], replicated, may hold values from 0 to 1, as said below
- driver: bfloat16 [1024, 1024], P(('pair', 'slab')), may hold values from -6 to 6
Outputs:
- residual: float32 [1024, 1024], P(('pair', 'slab'))
The draws below stay inside these ranges and needn't reach their ends.
Inputs may be any that keep to these rules, and one draw needn't show every extreme that they name: Each block carries an irreducible-representation label of 0 to 7; block_map[c, d] is 1 exactly where the labels of blocks c and d combine (bitwise exclusive or) to the window's label, which is not 0.
All inputs are finite; a program needn't handle non-finite values.
Results may differ from the reference program's by a relative error of at most 0.0003.
Values may be sent and summed in bfloat16 or wider, within the bound.
A program may use at most 128 MiB of HBM per device.

```python
import jax
import jax.numpy as jnp

V = 640
BLK = 64
AB = 1024
NB = 10
OP = 1024


def draw_block_map(key, part):
    key = jax.random.fold_in(key, 7)
    target_key, label_key, order_key = jax.random.split(key, 3)
    target = jax.random.randint(target_key, (), 1, 8).astype(jnp.int32)
    base = jax.random.randint(label_key, (NB // 2,), 0, 8).astype(jnp.int32)
    partner = jnp.bitwise_xor(base, target)
    paired = jnp.stack([base, partner], axis=1).reshape(NB)
    order = jax.random.permutation(order_key, NB).astype(jnp.int32)
    labels = paired[order]
    product = jnp.bitwise_xor(labels[:, None], labels[None, :])
    return (product == target).astype(jnp.int32)


def steps_of(own_key, dims, cuts, low, high):
    factor_of, own = 1.0, jax.random.fold_in(own_key, 6)
    for axis_at, shards_of in cuts:
        draws = jnp.exp(jax.random.uniform(jax.random.fold_in(own, axis_at), (shards_of,), jnp.float32, low / len(cuts), high / len(cuts)))
        factor_of = factor_of * jnp.repeat(draws, dims[axis_at] // shards_of).reshape([-1 if axis == axis_at else 1 for axis in range(len(dims))])
    return factor_of


def noise(key, dims, width, reach, shards=(), dtype=jnp.bfloat16):
    values = width * jax.random.normal(key, dims, jnp.float32)
    if shards:
        values = values * steps_of(key, dims, shards, -0.22, 0.18)
    return jnp.clip(values, -reach, reach).astype(dtype)


def setup_inputs(seed: int = 0) -> dict:
    key_list = jax.random.split(jax.random.key(seed), 5)
    amplitudes = noise(key_list[0], (OP, V, V), 1.0, 6.0, ((0, 8), (1, 32)))
    integrals = noise(key_list[1], (V, V, AB), (V * V // 2) ** -0.5, 0.013671875, ((0, 32), (1, 8)))
    block_map = draw_block_map(jax.random.fold_in(key_list[4], 71), 0)
    driver = noise(key_list[3], (OP, AB), 1.0, 6.0, ((0, 256),))
    return dict(amplitudes=amplitudes, integrals=integrals, block_map=block_map, driver=driver)


def reference(amplitudes, integrals, block_map, driver):
    blocks = jnp.arange(V) // BLK
    onehot = (blocks[:, None] == jnp.arange(V // BLK)[None, :]).astype(jnp.float32)
    allowed = jnp.dot(jnp.dot(onehot, block_map.astype(jnp.float32)), onehot.T).astype(jnp.bfloat16)
    masked = (integrals * allowed[:, :, None]).reshape(V * V, AB)
    ladder = jnp.dot(amplitudes.reshape(OP, V * V), masked, preferred_element_type=jnp.float32)
    return driver.astype(jnp.float32) + ladder
```

```python
import functools

import jax
import jax.numpy as jnp
from jax import lax
from jax.experimental import pallas as pl
from jax.experimental.pallas import tpu as pltpu
from jax.sharding import PartitionSpec as P

BLK = 64
HALF = 32
MESH = pl.DeviceIdType.MESH
F32, BF16 = jnp.float32, jnp.bfloat16


def tile_parts(q):
    return [[j for j in range(4) if q * j < 4 * t + 4 and q * j + q > 4 * t] for t in range(q)]


def kernel(
    q, a_hbm, i_hbm, bm, o_ref,
    a_v, i_v, pack, recv, sel, part, ybuf, zsend, zbuf, xsend, xbuf,
    a_sem, il_sem, is_sem, ir_sem, as_sem, ar_sem, ys_sem, yr_sem, zs_sem, zr_sem, xs_sem, xr_sem,
):
    pair, slab = lax.axis_index("pair"), lax.axis_index("slab")
    x, h, y, z = pair // 2, pair % 2, slab // 8, slab % 8
    n_groups = a_v.shape[0] // 4
    parts = tile_parts(q)
    first = [0]
    for p in parts:
        first.append(first[-1] + len(p))

    def at_x(d):
        return (lax.rem(x + d, 4) * 2 + h, slab)

    def at_y(d):
        return (pair, lax.rem(y + d, 4) * 8 + z)

    def at_z(d):
        return (pair, y * 8 + lax.rem(z + d, 8))

    other_core = (x * 2 + 1 - h, slab)

    def a_load(g):
        return pltpu.make_async_copy(a_hbm.at[pl.ds(4 * g, 4)], a_v.at[pl.ds(4 * g, 4)], a_sem.at[g])

    rows = pl.ds(pl.multiple_of(80 * h, 16), 80)
    i_local = pltpu.make_async_copy(i_hbm, i_v.at[:, rows], il_sem)
    i_remote = pltpu.make_async_remote_copy(
        i_hbm, i_v.at[:, rows], is_sem, ir_sem, device_id=other_core, device_id_type=MESH)

    for g in range(n_groups):
        a_load(g).start()
    i_local.start()

    barrier = pltpu.get_barrier_semaphore()
    peers = [at_x(d) for d in (1, 2, 3)] + [at_y(d) for d in (1, 2, 3)] + [at_z(d) for d in range(1, 8)]
    peers.append(other_core)
    for peer in peers:
        pl.semaphore_signal(barrier, inc=1, device_id=peer, device_id_type=MESH)

    block0 = (20 * slab) // BLK
    block1 = (20 * slab + 19) // BLK
    row = lax.broadcasted_iota(jnp.int32, (HALF, 128), 0)
    lane = lax.broadcasted_iota(jnp.int32, (HALF, 128), 1)
    diagonal = row == lane % HALF
    lane_unit = lane // HALF

    def build(which, block):
        def one(d, carry):
            k = lax.rem(x + d, 4)
            place = jnp.int32(0)
            for w in range(8):
                inside = jnp.where((w >= k) & (w < k + 5), 1, 0)
                blk = jnp.minimum(2 * k + w // 2, 9)
                ok = bm[block, blk] * inside
                if q == 5:
                    place = w - k
                for t in range(q):
                    for n, j in enumerate(parts[t]):
                        want = jnp.where(ok > 0, place + (q * j - 4 * t), -100)
                        ones = jnp.where(diagonal & (lane_unit == want), 1.0, 0.0).astype(BF16)
                        at = 256 * (first[t] + n) + HALF * w
                        sel[which, d, at:at + HALF, :] = ones
                if q != 5:
                    place = place + ok
            return carry
        lax.fori_loop(0, 4, one, 0)

    build(0, block0)

    @pl.when(block1 != block0)
    def _():
        build(1, block1)

    def pack_one(g, d):
        which = (20 * slab + 4 * g) // BLK - block0
        k = lax.rem(x + d, 4)
        window = pl.ds(pl.multiple_of(128 * k, 128), 256)
        for t in range(q):
            left = jnp.concatenate([a_v[4 * g + j, :, window] for j in parts[t]], axis=1)
            right = sel[which, d, 256 * first[t]:256 * first[t + 1], :]
            pack[d, g, t] = jnp.dot(left, right, preferred_element_type=F32).astype(BF16)

    def a_send(g, d):
        return pltpu.make_async_remote_copy(
            pack.at[d, g], recv.at[d - 1, g], as_sem.at[d - 1, g], ar_sem.at[d - 1, g],
            device_id=at_x(d), device_id_type=MESH)

    pl.semaphore_wait(barrier, len(peers))
    i_remote.start()

    def near(g, carry):
        a_load(g).wait()
        for d in (1, 3):
            pack_one(g, d)
            a_send(g, d).start()
        return carry

    lax.fori_loop(0, n_groups, near, 0)

    def far(g, carry):
        pack_one(g, 2)
        a_send(g, 2).start()
        return carry

    lax.fori_loop(0, n_groups, far, 0)

    def own(g, carry):
        pack_one(g, 0)
        return carry

    lax.fori_loop(0, n_groups, own, 0)
    i_local.wait()
    i_remote.wait()

    def multiply(d, g, held):
        left = jnp.concatenate([held[t] for t in range(q)], axis=1)
        right = i_v[pl.ds(4 * g, 4)].reshape(4 * i_v.shape[1], i_v.shape[2])
        term = jnp.dot(left, right, preferred_element_type=F32)

        @pl.when(g == 0)
        def _():
            part[d] = term

        @pl.when(g > 0)
        def _():
            part[d] += term

    def y_send(d, dy):
        to = lax.rem(y + dy, 4)
        return pltpu.make_async_remote_copy(
            part.at[d, pl.ds(pl.multiple_of(32 * to, 32), 32)], ybuf.at[d, dy - 1],
            ys_sem.at[d, dy - 1], yr_sem.at[d, dy - 1], device_id=at_y(dy), device_id_type=MESH)

    def z_send(d, dz):
        return pltpu.make_async_remote_copy(
            zsend.at[d, lax.rem(z + dz, 8)], zbuf.at[d, dz - 1],
            zs_sem.at[d, dz - 1], zr_sem.at[d, dz - 1], device_id=at_z(dz), device_id_type=MESH)

    def x_send(d):
        return pltpu.make_async_remote_copy(
            xsend.at[d], xbuf.at[d - 1], xs_sem.at[d - 1], xr_sem.at[d - 1],
            device_id=at_x(4 - d), device_id_type=MESH)

    def y_start(d):
        for dy in (2, 1, 3):
            y_send(d, dy).start()

    low = lax.broadcasted_iota(jnp.int32, (8, 512), 0) < 4

    def y_end(d):
        for dy in (1, 2, 3):
            y_send(d, dy).wait_recv()
        base = pl.multiple_of(32 * y, 32)
        for u in range(4):
            total = part[d, pl.ds(base + 8 * u, 8)]
            for dy in (1, 2, 3):
                total = total + ybuf[d, dy - 1, 8 * u:8 * u + 8]
            left, right = total[:, :512], total[:, 512:]
            zsend[d, 2 * u] = jnp.where(low, left, pltpu.roll(right, 4, 0))
            zsend[d, 2 * u + 1] = jnp.where(low, pltpu.roll(left, 4, 0), right)
        for dz in (4, 3, 5, 2, 6, 1, 7):
            z_send(d, dz).start()

    def z_end(d):
        for dz in range(1, 8):
            z_send(d, dz).wait_recv()
        total = zsend[d, z]
        for dz in range(1, 8):
            total = total + zbuf[d, dz - 1]
        xsend[d] = total
        if d:
            x_send(d).start()

    def own_product(g, carry):
        multiply(0, g, pack.at[0, g])
        return carry

    lax.fori_loop(0, n_groups, own_product, 0)
    y_start(0)
    y_end(0)

    def near_product(g, carry):
        for d in (1, 3):
            a_send(g, d).wait_recv()
            multiply(d, g, recv.at[d - 1, g])
        return carry

    lax.fori_loop(0, n_groups, near_product, 0)
    y_start(1)
    y_start(3)
    z_end(0)
    y_end(1)
    y_end(3)

    def far_product(g, carry):
        a_send(g, 2).wait_recv()
        multiply(2, g, recv.at[1, g])
        return carry

    lax.fori_loop(0, n_groups, far_product, 0)
    y_start(2)
    z_end(1)
    z_end(3)
    y_end(2)
    z_end(2)
    for d in (1, 3, 2):
        x_send(d).wait_recv()
    o_ref[...] = (xsend[0] + xbuf[0]) + (xbuf[1] + xbuf[2])

    def sent(g, carry):
        for d in (1, 2, 3):
            a_send(g, d).wait_send()
        return carry

    lax.fori_loop(0, n_groups, sent, 0)
    for d in range(4):
        for dy in (1, 2, 3):
            y_send(d, dy).wait_send()
        for dz in range(1, 8):
            z_send(d, dz).wait_send()
    for d in (1, 2, 3):
        x_send(d).wait_send()


def ladder_call(q, amps, ints, block_map):
    n_c, n_ij, n_d = amps.shape
    n_g = n_c // 4
    dma = pltpu.SemaphoreType.DMA
    return pl.pallas_call(
        functools.partial(kernel, q),
        out_shape=jax.ShapeDtypeStruct((8, 512), F32),
        in_specs=[
            pl.BlockSpec(memory_space=pl.ANY),
            pl.BlockSpec(memory_space=pl.ANY),
            pl.BlockSpec(memory_space=pltpu.SMEM),
        ],
        out_specs=pl.BlockSpec(memory_space=pltpu.VMEM),
        scratch_shapes=[
            pltpu.VMEM((n_c, n_ij, n_d), BF16),
            pltpu.VMEM((n_c, 160, 1024), BF16),
            pltpu.VMEM((4, n_g, q, 128, 128), BF16),
            pltpu.VMEM((3, n_g, q, 128, 128), BF16),
            pltpu.VMEM((2, 4, 256 * sum(map(len, tile_parts(q))), 128), BF16),
            pltpu.VMEM((4, 128, 1024), F32),
            pltpu.VMEM((4, 3, 32, 1024), F32),
            pltpu.VMEM((4, 8, 8, 512), F32),
            pltpu.VMEM((4, 7, 8, 512), F32),
            pltpu.VMEM((4, 8, 512), F32),
            pltpu.VMEM((3, 8, 512), F32),
            dma((n_g,)), dma, dma, dma,
            dma((3, n_g)), dma((3, n_g)),
            dma((4, 3)), dma((4, 3)),
            dma((4, 7)), dma((4, 7)),
            dma((3,)), dma((3,)),
        ],
        compiler_params=pltpu.CompilerParams(
            collective_id=q, has_side_effects=True, vmem_limit_bytes=56 * 2**20),
    )(amps, ints, block_map)


def on_device(amplitudes, integrals, block_map, driver):
    amps = jnp.transpose(amplitudes, (1, 0, 2))
    summed = ladder_call(5, amps, integrals, block_map)
    ladder = jnp.concatenate([summed[:4], summed[4:]], axis=1)
    return driver.astype(F32) + ladder


def solution(mesh):
    placed = (P("pair", "slab", None), P("slab", "pair", None), P(), P(("pair", "slab"), None))
    return jax.shard_map(
        on_device, mesh=mesh, in_specs=placed, out_specs=P(("pair", "slab"), None), check_vma=False
    )
```

```python
import functools

import jax
import jax.numpy as jnp
from jax import lax
from jax.experimental import pallas as pl
from jax.experimental.pallas import tpu as pltpu
from jax.sharding import PartitionSpec as P

BLK = 64
HALF = 32
MESH = pl.DeviceIdType.MESH
F32, BF16 = jnp.float32, jnp.bfloat16


def tile_parts(q):
    return [[j for j in range(4) if q * j < 4 * t + 4 and q * j + q > 4 * t] for t in range(q)]


def kernel(
    q, a_hbm, i_hbm, bm, o_ref,
    a_v, i_v, i_c, pack, recv, sel, part, ybuf1, ysend, ybuf2, zsend, zbuf, xsend, xbuf,
    a_sem, il_sem, is_sem, ir_sem, as_sem, ar_sem, y1s_sem, y1r_sem, y2s_sem, y2r_sem, zs_sem, zr_sem, xs_sem, xr_sem,
):
    pair, slab = lax.axis_index("pair"), lax.axis_index("slab")
    x, h, y, z = pair // 2, pair % 2, slab // 8, slab % 8
    n_groups = a_v.shape[0] // 4
    parts = tile_parts(q)
    first = [0]
    for p in parts:
        first.append(first[-1] + len(p))

    def at_x(d):
        return (lax.rem(x + d, 4) * 2 + h, slab)

    def across(side, at):
        return at + 1 - 2 * lax.rem(at, 2) if side == 0 else 3 - at

    def at_y(side):
        return (pair, across(side, y) * 8 + z)

    def at_z(d):
        return (pair, y * 8 + lax.rem(z + d, 8))

    other_core = (x * 2 + 1 - h, slab)

    def a_load(g):
        return pltpu.make_async_copy(a_hbm.at[pl.ds(4 * g, 4)], a_v.at[pl.ds(4 * g, 4)], a_sem.at[g])

    rows = pl.ds(pl.multiple_of(80 * h, 16), 80)

    def i_local(g):
        chunk = pl.ds(4 * g, 4)
        return pltpu.make_async_copy(i_hbm.at[chunk], i_v.at[chunk, rows], il_sem.at[g])

    def i_remote(g):
        chunk = pl.ds(4 * g, 4)
        return pltpu.make_async_remote_copy(
            i_hbm.at[chunk], i_v.at[chunk, rows], is_sem, ir_sem.at[g],
            device_id=other_core, device_id_type=MESH)

    for g in range(n_groups):
        a_load(g).start()
    for g in range(n_groups):
        i_local(g).start()

    barrier = pltpu.get_barrier_semaphore()
    peers = [at_x(d) for d in (1, 2, 3)] + [at_y(0), at_y(1)] + [at_z(d) for d in range(1, 8)]
    peers.append(other_core)
    for peer in peers:
        pl.semaphore_signal(barrier, inc=1, device_id=peer, device_id_type=MESH)

    block0 = (20 * slab) // BLK
    block1 = (20 * slab + 19) // BLK
    row = lax.broadcasted_iota(jnp.int32, (HALF, 128), 0)
    lane = lax.broadcasted_iota(jnp.int32, (HALF, 128), 1)
    diagonal = row == lane % HALF
    lane_unit = lane // HALF

    def build(which, block):
        def one(d, carry):
            k = lax.rem(x + d, 4)
            place = jnp.int32(0)
            for w in range(8):
                inside = jnp.where((w >= k) & (w < k + 5), 1, 0)
                blk = jnp.minimum(2 * k + w // 2, 9)
                ok = bm[block, blk] * inside
                if q == 5:
                    place = w - k
                for t in range(q):
                    for n, j in enumerate(parts[t]):
                        want = jnp.where(ok > 0, place + (q * j - 4 * t), -100)
                        ones = jnp.where(diagonal & (lane_unit == want), 1.0, 0.0).astype(BF16)
                        at = 256 * (first[t] + n) + HALF * w
                        sel[which, d, at:at + HALF, :] = ones
                if q != 5:
                    place = place + ok
            return carry
        lax.fori_loop(0, 4, one, 0)

    build(0, block0)

    @pl.when(block1 != block0)
    def _():
        build(1, block1)

    def pack_one(g, d):
        which = (20 * slab + 4 * g) // BLK - block0
        k = lax.rem(x + d, 4)
        window = pl.ds(pl.multiple_of(128 * k, 128), 256)
        for t in range(q):
            left = jnp.concatenate([a_v[4 * g + j, :, window] for j in parts[t]], axis=1)
            right = sel[which, d, 256 * first[t]:256 * first[t + 1], :]
            pack[d, g, t] = jnp.dot(left, right, preferred_element_type=F32).astype(BF16)

    def a_send(g, d):
        return pltpu.make_async_remote_copy(
            pack.at[d, g], recv.at[d - 1, g], as_sem, ar_sem.at[d - 1, g],
            device_id=at_x(d), device_id_type=MESH)

    pl.semaphore_wait(barrier, len(peers))
    for g in range(n_groups):
        i_remote(g).start()

    def near(g, carry):
        a_load(g).wait()
        for d in (1, 3):
            pack_one(g, d)
            a_send(g, d).start()
        return carry

    lax.fori_loop(0, n_groups, near, 0)

    def squeeze(g):
        block = (20 * slab + 4 * g) // BLK
        place = jnp.int32(0)
        weight = [{} for _ in range(q)]
        for e in range(5):
            ok = bm[block, (5 * x + e) // 2]
            for t in range(min(q, e + 1)):
                chosen = jnp.where((ok > 0) & (place == t), 1.0, 0.0)
                weight[t][e] = jnp.full((HALF, 1024), chosen, F32).astype(BF16)
            place = place + ok
        for j in range(4):
            for t in range(q):
                total = None
                for e, w in weight[t].items():
                    term = i_v[4 * g + j, HALF * e:HALF * e + HALF, :] * w
                    total = term if total is None else total + term
                i_c[4 * g + j, HALF * t:HALF * t + HALF, :] = total

    held_i = i_v if q == 5 else i_c

    def multiply(g, held):
        left = jnp.concatenate(
            [jnp.concatenate([tiles[t] for t in range(q)], axis=1) for _, tiles in held], axis=0)
        right = held_i[pl.ds(4 * g, 4)].reshape(4 * HALF * q, held_i.shape[2])
        term = jnp.dot(left, right, preferred_element_type=F32)
        for at, (d, _) in enumerate(held):
            for half in range(2):
                cols = term[128 * at:128 * at + 128, 512 * half:512 * half + 512]

                @pl.when(g == 0)
                def _():
                    part[d, half] = cols

                @pl.when(g > 0)
                def _():
                    part[d, half] += cols

    def y_rows(at):
        return pl.ds(pl.multiple_of(32 * at, 32), 32)

    def y1_send(d, half, slot):
        to = across(half, y)
        rows_of = to if slot == 0 else across(1 - half, to)
        return pltpu.make_async_remote_copy(
            part.at[d, half, y_rows(rows_of)], ybuf1.at[d, half, slot],
            y1s_sem, y1r_sem.at[d, half, slot],
            device_id=at_y(half), device_id_type=MESH)

    def y2_send(d, half):
        return pltpu.make_async_remote_copy(
            ysend.at[d, half], ybuf2.at[d, half], y2s_sem, y2r_sem.at[d, half],
            device_id=at_y(1 - half), device_id_type=MESH)

    def z_send(d, dz):
        return pltpu.make_async_remote_copy(
            zsend.at[d, lax.rem(z + dz, 8)], zbuf.at[d, dz - 1], zs_sem, zr_sem.at[d],
            device_id=at_z(dz), device_id_type=MESH)

    def drain(ref, sem):
        pltpu.make_async_copy(ref, ref, sem).wait()

    def x_send(d):
        return pltpu.make_async_remote_copy(
            xsend.at[d], xbuf.at[d - 1], xs_sem, xr_sem,
            device_id=at_x(4 - d), device_id_type=MESH)

    def y1_start(d):
        for slot in (1, 0):
            for half in (0, 1):
                y1_send(d, half, slot).start()

    def y2_start(d):
        for half in (0, 1):
            y1_send(d, half, 1).wait_recv()
            ysend[d, half] = part[d, half, y_rows(across(1 - half, y))] + ybuf1[d, half, 1]
            y2_send(d, half).start()

    low = lax.broadcasted_iota(jnp.int32, (8, 512), 0) < 4

    def z_start(d):
        for half in (0, 1):
            y1_send(d, half, 0).wait_recv()
            y2_send(d, half).wait_recv()
        base = pl.multiple_of(32 * y, 32)
        for u in range(4):
            left, right = [
                part[d, half, pl.ds(base + 8 * u, 8)]
                + (ybuf1[d, half, 0, 8 * u:8 * u + 8] + ybuf2[d, half, 8 * u:8 * u + 8])
                for half in (0, 1)
            ]
            zsend[d, 2 * u] = jnp.where(low, left, pltpu.roll(right, 4, 0))
            zsend[d, 2 * u + 1] = jnp.where(low, pltpu.roll(left, 4, 0), right)
        for dz in (4, 3, 5, 2, 6, 1, 7):
            z_send(d, dz).start()

    def z_end(d):
        drain(zbuf.at[d], zr_sem.at[d])
        total = zsend[d, z]
        for dz in range(1, 8):
            total = total + zbuf[d, dz - 1]
        xsend[d] = total
        if d:
            x_send(d).start()

    def own(g, carry):
        pack_one(g, 0)
        i_local(g).wait()
        i_remote(g).wait_recv()
        if q != 5:
            squeeze(g)
        multiply(g, [(0, pack.at[0, g])])
        return carry

    def far(g, carry):
        pack_one(g, 2)
        a_send(g, 2).start()
        return carry

    def near_product(g, carry):
        for d in (1, 3):
            a_send(g, d).wait_recv()
        multiply(g, [(1, recv.at[0, g]), (3, recv.at[2, g])])
        return carry

    def far_product(g, carry):
        a_send(g, 2).wait_recv()
        multiply(g, [(2, recv.at[1, g])])
        return carry

    lax.fori_loop(0, n_groups, own, 0)
    y1_start(0)
    lax.fori_loop(0, n_groups, far, 0)
    if q > 2:
        y2_start(0)
    lax.fori_loop(0, n_groups, near_product, 0)
    y1_start(1)
    y1_start(3)
    if q == 2:
        y2_start(0)
        y2_start(1)
    else:
        z_start(0)
        y2_start(1)
        y2_start(3)
    if q > 3:
        z_start(1)
        z_start(3)
        z_end(0)
        z_end(1)
        z_end(3)
    lax.fori_loop(0, n_groups, far_product, 0)
    y1_start(2)
    if q == 2:
        y2_start(3)
        z_start(0)
    if q <= 3:
        z_start(1)
        z_start(3)
    y2_start(2)
    if q <= 3:
        z_end(0)
    z_start(2)
    if q <= 3:
        z_end(1)
        z_end(3)
    z_end(2)
    drain(xbuf, xr_sem)
    o_ref[...] = (xsend[0] + xbuf[0]) + (xbuf[1] + xbuf[2])
    drain(i_v.at[:, pl.ds(0, 80)], is_sem)
    drain(recv, as_sem)
    drain(ybuf1, y1s_sem)
    drain(ybuf2, y2s_sem)
    drain(zbuf, zs_sem)
    drain(xbuf, xs_sem)


def ladder_call(q, amps, ints, block_map):
    n_c, n_ij, n_d = amps.shape
    n_g = n_c // 4
    dma = pltpu.SemaphoreType.DMA
    return pl.pallas_call(
        functools.partial(kernel, q),
        out_shape=jax.ShapeDtypeStruct((8, 512), F32),
        in_specs=[
            pl.BlockSpec(memory_space=pl.ANY),
            pl.BlockSpec(memory_space=pl.ANY),
            pl.BlockSpec(memory_space=pltpu.SMEM),
        ],
        out_specs=pl.BlockSpec(memory_space=pltpu.VMEM),
        scratch_shapes=[
            pltpu.VMEM((n_c, n_ij, n_d), BF16),
            pltpu.VMEM((n_c, 160, 1024), BF16),
            pltpu.VMEM((n_c if q != 5 else 1, HALF * q, 1024), BF16),
            pltpu.VMEM((4, n_g, q, 128, 128), BF16),
            pltpu.VMEM((3, n_g, q, 128, 128), BF16),
            pltpu.VMEM((2, 4, 256 * sum(map(len, tile_parts(q))), 128), BF16),
            pltpu.VMEM((4, 2, 128, 512), F32),
            pltpu.VMEM((4, 2, 2, 32, 512), F32),
            pltpu.VMEM((4, 2, 32, 512), F32),
            pltpu.VMEM((4, 2, 32, 512), F32),
            pltpu.VMEM((4, 8, 8, 512), F32),
            pltpu.VMEM((4, 7, 8, 512), F32),
            pltpu.VMEM((4, 8, 512), F32),
            pltpu.VMEM((3, 8, 512), F32),
            dma((n_g,)), dma((n_g,)), dma, dma((n_g,)),
            dma, dma((3, n_g)),
            dma, dma((4, 2, 2)),
            dma, dma((4, 2)),
            dma, dma((4,)),
            dma, dma,
        ],
        compiler_params=pltpu.CompilerParams(
            collective_id=q, has_side_effects=True, vmem_limit_bytes=56 * 2**20),
    )(amps, ints, block_map)


def on_device(amplitudes, integrals, block_map, driver):
    amps = jnp.transpose(amplitudes, (1, 0, 2))
    shares = jnp.repeat(block_map, 2, axis=1).reshape(block_map.shape[0], 4, 5).sum(axis=2)
    need = jnp.clip(jnp.max(shares), 2, 5)
    summed = lax.switch(
        need - 2, [functools.partial(ladder_call, q) for q in (2, 3, 4, 5)], amps, integrals, block_map)
    ladder = jnp.concatenate([summed[:4], summed[4:]], axis=1)
    return driver.astype(F32) + ladder


def solution(mesh):
    placed = (P("pair", "slab", None), P("slab", "pair", None), P(), P(("pair", "slab"), None))
    return jax.shard_map(
        on_device, mesh=mesh, in_specs=placed, out_specs=P(("pair", "slab"), None), check_vma=False
    )
```

```python
import functools

import jax
import jax.numpy as jnp
from jax import lax
from jax.experimental import pallas as pl
from jax.experimental.pallas import tpu as pltpu
from jax.sharding import PartitionSpec as P

BLK = 64
HALF = 32
MESH = pl.DeviceIdType.MESH
F32, BF16 = jnp.float32, jnp.bfloat16


START = [("own",), ("y1", 0), ("far",)]
ORDER = {
    2: [
        ("far",), ("own",), ("y1", 0),
        ("near_product",), ("y1", 1), ("y1", 3), ("y2", 0), ("y2", 1),
        ("far_product",), ("y1", 2), ("y2", 3), ("z", 0), ("z", 1), ("y2", 2),
        ("z", 3), ("z", 2), ("x", 0), ("x", 1), ("x", 3), ("x", 2),
    ],
    3: START + [
        ("y2", 0), ("near_product",), ("y1", 1), ("y1", 3), ("z", 0), ("y2", 1), ("y2", 3),
        ("far_product",), ("y1", 2), ("z", 1), ("z", 3), ("y2", 2),
        ("x", 0), ("z", 2), ("x", 1), ("x", 3), ("x", 2),
    ],
    4: START + [
        ("y2", 0), ("near_product",), ("y1", 1), ("y1", 3), ("z", 0), ("y2", 1), ("y2", 3),
        ("z", 1), ("z", 3), ("far_product",), ("y1", 2), ("y2", 2),
        ("x", 0), ("z", 2), ("x", 1), ("x", 3), ("x", 2),
    ],
}
ORDER[5] = ORDER[4]


def tile_parts(q):
    return [[j for j in range(4) if q * j < 4 * t + 4 and q * j + q > 4 * t] for t in range(q)]


def kernel(
    q, a_hbm, i_hbm, bm, o_ref,
    a_v, i_v, i_c, pack, recv, sel, part, ybuf1, ysend, ybuf2, zsend, zbuf, xsend, xbuf,
    a_sem, il_sem, is_sem, ir_sem, as_sem, ar_sem, y1s_sem, y1r_sem, y2s_sem, y2r_sem, zs_sem, zr_sem, xs_sem, xr_sem,
):
    pair, slab = lax.axis_index("pair"), lax.axis_index("slab")
    x, h, y, z = pair // 2, pair % 2, slab // 8, slab % 8
    n_groups = a_v.shape[0] // 4
    parts = tile_parts(q)
    first = [0]
    for p in parts:
        first.append(first[-1] + len(p))

    def at_x(d):
        return (lax.rem(x + d, 4) * 2 + h, slab)

    def across(side, at):
        return at + 1 - 2 * lax.rem(at, 2) if side == 0 else 3 - at

    def at_y(side):
        return (pair, across(side, y) * 8 + z)

    def at_z(d):
        return (pair, y * 8 + lax.rem(z + d, 8))

    other_core = (x * 2 + 1 - h, slab)

    def a_load(g):
        return pltpu.make_async_copy(a_hbm.at[pl.ds(4 * g, 4)], a_v.at[pl.ds(4 * g, 4)], a_sem.at[g])

    rows = pl.ds(pl.multiple_of(80 * h, 16), 80)

    def i_local(g):
        chunk = pl.ds(4 * g, 4)
        return pltpu.make_async_copy(i_hbm.at[chunk], i_v.at[chunk, rows], il_sem.at[g])

    def i_remote(g):
        chunk = pl.ds(4 * g, 4)
        return pltpu.make_async_remote_copy(
            i_hbm.at[chunk], i_v.at[chunk, rows], is_sem, ir_sem.at[g],
            device_id=other_core, device_id_type=MESH)

    for g in range(n_groups):
        a_load(g).start()
    for g in range(n_groups):
        i_local(g).start()

    barrier = pltpu.get_barrier_semaphore()
    peers = [at_x(d) for d in (1, 2, 3)] + [at_y(0), at_y(1)] + [at_z(d) for d in range(1, 8)]
    peers.append(other_core)
    for peer in peers:
        pl.semaphore_signal(barrier, inc=1, device_id=peer, device_id_type=MESH)

    block0 = (20 * slab) // BLK
    block1 = (20 * slab + 19) // BLK
    row = lax.broadcasted_iota(jnp.int32, (HALF, 128), 0)
    lane = lax.broadcasted_iota(jnp.int32, (HALF, 128), 1)
    diagonal = row == lane % HALF
    lane_unit = lane // HALF

    def build(which, block):
        def one(d, carry):
            k = lax.rem(x + d, 4)
            place = jnp.int32(0)
            for w in range(8):
                inside = jnp.where((w >= k) & (w < k + 5), 1, 0)
                blk = jnp.minimum(2 * k + w // 2, 9)
                ok = bm[block, blk] * inside
                if q == 5:
                    place = w - k
                for t in range(q):
                    for n, j in enumerate(parts[t]):
                        want = jnp.where(ok > 0, place + (q * j - 4 * t), -100)
                        ones = jnp.where(diagonal & (lane_unit == want), 1.0, 0.0).astype(BF16)
                        at = 256 * (first[t] + n) + HALF * w
                        sel[which, d, at:at + HALF, :] = ones
                if q != 5:
                    place = place + ok
            return carry
        lax.fori_loop(0, 4, one, 0)

    build(0, block0)

    @pl.when(block1 != block0)
    def _():
        build(1, block1)

    def pack_one(g, d):
        which = (20 * slab + 4 * g) // BLK - block0
        k = lax.rem(x + d, 4)
        window = pl.ds(pl.multiple_of(128 * k, 128), 256)
        for t in range(q):
            left = jnp.concatenate([a_v[4 * g + j, :, window] for j in parts[t]], axis=1)
            right = sel[which, d, 256 * first[t]:256 * first[t + 1], :]
            pack[d, g, t] = jnp.dot(left, right, preferred_element_type=F32).astype(BF16)

    def a_send(g, d):
        return pltpu.make_async_remote_copy(
            pack.at[d, g], recv.at[d - 1, g], as_sem, ar_sem.at[d - 1, g],
            device_id=at_x(d), device_id_type=MESH)

    pl.semaphore_wait(barrier, len(peers))
    for g in range(n_groups):
        i_remote(g).start()

    def near(g, carry):
        a_load(g).wait()
        for d in (1, 3):
            pack_one(g, d)
            a_send(g, d).start()
        return carry

    lax.fori_loop(0, n_groups, near, 0)

    def squeeze(g):
        block = (20 * slab + 4 * g) // BLK
        place = jnp.int32(0)
        weight = [{} for _ in range(q)]
        for e in range(5):
            ok = bm[block, (5 * x + e) // 2]
            for t in range(min(q, e + 1)):
                chosen = jnp.where((ok > 0) & (place == t), 1.0, 0.0)
                weight[t][e] = jnp.full((HALF, 1024), chosen, F32).astype(BF16)
            place = place + ok
        for j in range(4):
            for t in range(q):
                total = None
                for e, w in weight[t].items():
                    term = i_v[4 * g + j, HALF * e:HALF * e + HALF, :] * w
                    total = term if total is None else total + term
                i_c[4 * g + j, HALF * t:HALF * t + HALF, :] = total

    held_i = i_v if q == 5 else i_c

    def multiply(g, held):
        left = jnp.concatenate(
            [jnp.concatenate([tiles[t] for t in range(q)], axis=1) for _, tiles in held], axis=0)
        right = held_i[pl.ds(4 * g, 4)].reshape(4 * HALF * q, held_i.shape[2])
        term = jnp.dot(left, right, preferred_element_type=F32)
        for at, (d, _) in enumerate(held):
            for half in range(2):
                cols = term[128 * at:128 * at + 128, 512 * half:512 * half + 512]

                @pl.when(g == 0)
                def _():
                    part[d, half] = cols

                @pl.when(g > 0)
                def _():
                    part[d, half] += cols

    def y_rows(at):
        return pl.ds(pl.multiple_of(32 * at, 32), 32)

    def y1_send(d, half, slot):
        to = across(half, y)
        rows_of = to if slot == 0 else across(1 - half, to)
        return pltpu.make_async_remote_copy(
            part.at[d, half, y_rows(rows_of)], ybuf1.at[d, half, slot],
            y1s_sem, y1r_sem.at[d, half, slot],
            device_id=at_y(half), device_id_type=MESH)

    def y2_send(d, half):
        return pltpu.make_async_remote_copy(
            ysend.at[d, half], ybuf2.at[d, half], y2s_sem, y2r_sem.at[d, half],
            device_id=at_y(1 - half), device_id_type=MESH)

    def z_send(d, dz):
        return pltpu.make_async_remote_copy(
            zsend.at[d, lax.rem(z + dz, 8)], zbuf.at[d, dz - 1], zs_sem, zr_sem.at[d],
            device_id=at_z(dz), device_id_type=MESH)

    def drain(ref, sem):
        pltpu.make_async_copy(ref, ref, sem).wait()

    def x_send(d):
        return pltpu.make_async_remote_copy(
            xsend.at[d], xbuf.at[d - 1], xs_sem, xr_sem,
            device_id=at_x(4 - d), device_id_type=MESH)

    def y1_start(d):
        for slot in (1, 0):
            for half in (0, 1):
                y1_send(d, half, slot).start()

    def y2_start(d):
        for half in (0, 1):
            y1_send(d, half, 1).wait_recv()
            ysend[d, half] = part[d, half, y_rows(across(1 - half, y))] + ybuf1[d, half, 1]
            y2_send(d, half).start()

    low = lax.broadcasted_iota(jnp.int32, (8, 512), 0) < 4

    def z_start(d):
        for half in (0, 1):
            y1_send(d, half, 0).wait_recv()
            y2_send(d, half).wait_recv()
        base = pl.multiple_of(32 * y, 32)
        for u in range(4):
            left, right = [
                part[d, half, pl.ds(base + 8 * u, 8)]
                + (ybuf1[d, half, 0, 8 * u:8 * u + 8] + ybuf2[d, half, 8 * u:8 * u + 8])
                for half in (0, 1)
            ]
            zsend[d, 2 * u] = jnp.where(low, left, pltpu.roll(right, 4, 0))
            zsend[d, 2 * u + 1] = jnp.where(low, pltpu.roll(left, 4, 0), right)
        for dz in (4, 3, 5, 2, 6, 1, 7):
            z_send(d, dz).start()

    def z_end(d):
        drain(zbuf.at[d], zr_sem.at[d])
        total = zsend[d, z]
        for dz in range(1, 8):
            total = total + zbuf[d, dz - 1]
        xsend[d] = total
        if d:
            x_send(d).start()

    def own(g, carry):
        pack_one(g, 0)
        i_local(g).wait()
        i_remote(g).wait_recv()
        if q != 5:
            squeeze(g)
        multiply(g, [(0, pack.at[0, g])])
        return carry

    def far(g, carry):
        pack_one(g, 2)
        a_send(g, 2).start()
        return carry

    def near_product(g, carry):
        for d in (1, 3):
            a_send(g, d).wait_recv()
        multiply(g, [(1, recv.at[0, g]), (3, recv.at[2, g])])
        return carry

    def far_product(g, carry):
        a_send(g, 2).wait_recv()
        multiply(g, [(2, recv.at[1, g])])
        return carry

    run = {
        "own": lambda: lax.fori_loop(0, n_groups, own, 0),
        "far": lambda: lax.fori_loop(0, n_groups, far, 0),
        "near_product": lambda: lax.fori_loop(0, n_groups, near_product, 0),
        "far_product": lambda: lax.fori_loop(0, n_groups, far_product, 0),
        "y1": y1_start, "y2": y2_start, "z": z_start, "x": z_end,
    }
    for name, *group in ORDER[q]:
        run[name](*group)
    drain(xbuf, xr_sem)
    o_ref[...] = (xsend[0] + xbuf[0]) + (xbuf[1] + xbuf[2])
    drain(i_v.at[:, pl.ds(0, 80)], is_sem)
    drain(recv, as_sem)
    drain(ybuf1, y1s_sem)
    drain(ybuf2, y2s_sem)
    drain(zbuf, zs_sem)
    drain(xbuf, xs_sem)


def ladder_call(q, amps, ints, block_map):
    n_c, n_ij, n_d = amps.shape
    n_g = n_c // 4
    dma = pltpu.SemaphoreType.DMA
    return pl.pallas_call(
        functools.partial(kernel, q),
        out_shape=jax.ShapeDtypeStruct((8, 512), F32),
        in_specs=[
            pl.BlockSpec(memory_space=pl.ANY),
            pl.BlockSpec(memory_space=pl.ANY),
            pl.BlockSpec(memory_space=pltpu.SMEM),
        ],
        out_specs=pl.BlockSpec(memory_space=pltpu.VMEM),
        scratch_shapes=[
            pltpu.VMEM((n_c, n_ij, n_d), BF16),
            pltpu.VMEM((n_c, 160, 1024), BF16),
            pltpu.VMEM((n_c if q != 5 else 1, HALF * q, 1024), BF16),
            pltpu.VMEM((4, n_g, q, 128, 128), BF16),
            pltpu.VMEM((3, n_g, q, 128, 128), BF16),
            pltpu.VMEM((2, 4, 256 * sum(map(len, tile_parts(q))), 128), BF16),
            pltpu.VMEM((4, 2, 128, 512), F32),
            pltpu.VMEM((4, 2, 2, 32, 512), F32),
            pltpu.VMEM((4, 2, 32, 512), F32),
            pltpu.VMEM((4, 2, 32, 512), F32),
            pltpu.VMEM((4, 8, 8, 512), F32),
            pltpu.VMEM((4, 7, 8, 512), F32),
            pltpu.VMEM((4, 8, 512), F32),
            pltpu.VMEM((3, 8, 512), F32),
            dma((n_g,)), dma((n_g,)), dma, dma((n_g,)),
            dma, dma((3, n_g)),
            dma, dma((4, 2, 2)),
            dma, dma((4, 2)),
            dma, dma((4,)),
            dma, dma,
        ],
        compiler_params=pltpu.CompilerParams(
            collective_id=q, has_side_effects=True, vmem_limit_bytes=56 * 2**20),
    )(amps, ints, block_map)


def on_device(amplitudes, integrals, block_map, driver):
    amps = jnp.transpose(amplitudes, (1, 0, 2))
    shares = jnp.repeat(block_map, 2, axis=1).reshape(block_map.shape[0], 4, 5).sum(axis=2)
    need = jnp.clip(jnp.max(shares), 2, 5)
    summed = lax.switch(
        need - 2, [functools.partial(ladder_call, q) for q in (2, 3, 4, 5)], amps, integrals, block_map)
    ladder = jnp.concatenate([summed[:4], summed[4:]], axis=1)
    return driver.astype(F32) + ladder


def solution(mesh):
    placed = (P("pair", "slab", None), P("slab", "pair", None), P(), P(("pair", "slab"), None))
    return jax.shard_map(
        on_device, mesh=mesh, in_specs=placed, out_specs=P(("pair", "slab"), None), check_vma=False
    )
```

```python
import functools

import jax
import jax.numpy as jnp
from jax import lax
from jax.experimental import pallas as pl
from jax.experimental.pallas import tpu as pltpu
from jax.sharding import PartitionSpec as P

BLK = 64
HALF = 32
MESH = pl.DeviceIdType.MESH
F32, BF16 = jnp.float32, jnp.bfloat16


START = [("own",), ("y1", 0), ("far",)]
ORDER = {
    2: [
        ("far",), ("own",), ("y1", 0),
        ("near_product",), ("y1", 1), ("y1", 3), ("y2", 0), ("y2", 1),
        ("far_product",), ("far_end",), ("y2", 3), ("z", 0), ("z", 1), ("y2", 2),
        ("z", 3), ("z", 2), ("x", 0), ("x", 1), ("x", 3), ("x", 2),
    ],
    3: START + [
        ("y2", 0), ("near_product",), ("y1", 1), ("y1", 3), ("z", 0), ("y2", 1), ("y2", 3),
        ("far_product",), ("far_end",), ("z", 1), ("z", 3), ("y2", 2),
        ("x", 0), ("z", 2), ("x", 1), ("x", 3), ("x", 2),
    ],
    4: START + [
        ("y2", 0), ("near_product",), ("y1", 1), ("y1", 3), ("z", 0), ("y2", 1), ("y2", 3),
        ("z", 1), ("z", 3), ("far_product",), ("far_end",), ("y2", 2),
        ("x", 0), ("z", 2), ("x", 1), ("x", 3), ("x", 2),
    ],
}
ORDER[5] = ORDER[4]


def tile_parts(q):
    return [[j for j in range(4) if q * j < 4 * t + 4 and q * j + q > 4 * t] for t in range(q)]


def kernel(
    q, a_hbm, i_hbm, bm, o_ref,
    a_v, i_v, i_c, pack, recv, sel, part, ybuf1, ysend, ybuf2, zsend, zbuf, xsend, xbuf,
    a_sem, il_sem, is_sem, ir_sem, as_sem, ar_sem, y1s_sem, y1r_sem, y2s_sem, y2r_sem, zs_sem, zr_sem, xs_sem, xr_sem,
):
    pair, slab = lax.axis_index("pair"), lax.axis_index("slab")
    x, h, y, z = pair // 2, pair % 2, slab // 8, slab % 8
    n_groups = a_v.shape[0] // 4
    parts = tile_parts(q)
    first = [0]
    for p in parts:
        first.append(first[-1] + len(p))

    def at_x(d):
        return (lax.rem(x + d, 4) * 2 + h, slab)

    def across(side, at):
        return at + 1 - 2 * lax.rem(at, 2) if side == 0 else 3 - at

    def at_y(side):
        return (pair, across(side, y) * 8 + z)

    def at_z(d):
        return (pair, y * 8 + lax.rem(z + d, 8))

    other_core = (x * 2 + 1 - h, slab)

    def a_load(g):
        return pltpu.make_async_copy(a_hbm.at[pl.ds(4 * g, 4)], a_v.at[pl.ds(4 * g, 4)], a_sem.at[g])

    rows = pl.ds(pl.multiple_of(80 * h, 16), 80)

    def i_local(g):
        chunk = pl.ds(4 * g, 4)
        return pltpu.make_async_copy(i_hbm.at[chunk], i_v.at[chunk, rows], il_sem.at[g])

    def i_remote(g):
        chunk = pl.ds(4 * g, 4)
        return pltpu.make_async_remote_copy(
            i_hbm.at[chunk], i_v.at[chunk, rows], is_sem, ir_sem.at[g],
            device_id=other_core, device_id_type=MESH)

    for g in range(n_groups):
        a_load(g).start()
    for g in range(n_groups):
        i_local(g).start()

    barrier = pltpu.get_barrier_semaphore()
    peers = [at_x(d) for d in (1, 2, 3)] + [at_y(0), at_y(1)] + [at_z(d) for d in range(1, 8)]
    peers.append(other_core)
    for peer in peers:
        pl.semaphore_signal(barrier, inc=1, device_id=peer, device_id_type=MESH)

    block0 = (20 * slab) // BLK
    block1 = (20 * slab + 19) // BLK
    row = lax.broadcasted_iota(jnp.int32, (HALF, 128), 0)
    lane = lax.broadcasted_iota(jnp.int32, (HALF, 128), 1)
    diagonal = row == lane % HALF
    lane_unit = lane // HALF

    def build(which, block):
        def one(d, carry):
            k = lax.rem(x + d, 4)
            place = jnp.int32(0)
            for w in range(8):
                inside = jnp.where((w >= k) & (w < k + 5), 1, 0)
                blk = jnp.minimum(2 * k + w // 2, 9)
                ok = bm[block, blk] * inside
                if q == 5:
                    place = w - k
                for t in range(q):
                    for n, j in enumerate(parts[t]):
                        want = jnp.where(ok > 0, place + (q * j - 4 * t), -100)
                        ones = jnp.where(diagonal & (lane_unit == want), 1.0, 0.0).astype(BF16)
                        at = 256 * (first[t] + n) + HALF * w
                        sel[which, d, at:at + HALF, :] = ones
                if q != 5:
                    place = place + ok
            return carry
        lax.fori_loop(0, 4, one, 0)

    build(0, block0)

    @pl.when(block1 != block0)
    def _():
        build(1, block1)

    def pack_one(g, d):
        which = (20 * slab + 4 * g) // BLK - block0
        k = lax.rem(x + d, 4)
        window = pl.ds(pl.multiple_of(128 * k, 128), 256)
        for t in range(q):
            left = jnp.concatenate([a_v[4 * g + j, :, window] for j in parts[t]], axis=1)
            right = sel[which, d, 256 * first[t]:256 * first[t + 1], :]
            pack[d, g, t] = jnp.dot(left, right, preferred_element_type=F32).astype(BF16)

    def a_send(g, d):
        return pltpu.make_async_remote_copy(
            pack.at[d, g], recv.at[d - 1, g], as_sem, ar_sem.at[d - 1, g],
            device_id=at_x(d), device_id_type=MESH)

    pl.semaphore_wait(barrier, len(peers))
    for g in range(n_groups):
        i_remote(g).start()

    def near(g, carry):
        a_load(g).wait()
        for d in (1, 3):
            pack_one(g, d)
            a_send(g, d).start()
        return carry

    lax.fori_loop(0, n_groups, near, 0)

    def squeeze(g):
        block = (20 * slab + 4 * g) // BLK
        place = jnp.int32(0)
        weight = [{} for _ in range(q)]
        for e in range(5):
            ok = bm[block, (5 * x + e) // 2]
            for t in range(min(q, e + 1)):
                chosen = jnp.where((ok > 0) & (place == t), 1.0, 0.0)
                weight[t][e] = jnp.full((HALF, 1024), chosen, F32).astype(BF16)
            place = place + ok
        for j in range(4):
            for t in range(q):
                total = None
                for e, w in weight[t].items():
                    term = i_v[4 * g + j, HALF * e:HALF * e + HALF, :] * w
                    total = term if total is None else total + term
                i_c[4 * g + j, HALF * t:HALF * t + HALF, :] = total

    held_i = i_v if q == 5 else i_c

    def multiply(g, held):
        left = jnp.concatenate(
            [jnp.concatenate([tiles[t] for t in range(q)], axis=1) for _, tiles in held], axis=0)
        right = held_i[pl.ds(4 * g, 4)].reshape(4 * HALF * q, held_i.shape[2])
        term = jnp.dot(left, right, preferred_element_type=F32)
        for at, (d, _) in enumerate(held):
            for half in range(2):
                cols = term[128 * at:128 * at + 128, 512 * half:512 * half + 512]

                @pl.when(g == 0)
                def _():
                    part[d, half] = cols

                @pl.when(g > 0)
                def _():
                    part[d, half] += cols

    def y_rows(at):
        return pl.ds(pl.multiple_of(32 * at, 32), 32)

    def y1_send(d, half, slot):
        to = across(half, y)
        rows_of = to if slot == 0 else across(1 - half, to)
        return pltpu.make_async_remote_copy(
            part.at[d, half, y_rows(rows_of)], ybuf1.at[d, half, slot],
            y1s_sem, y1r_sem.at[d, half, slot],
            device_id=at_y(half), device_id_type=MESH)

    def y2_send(d, half):
        return pltpu.make_async_remote_copy(
            ysend.at[d, half], ybuf2.at[d, half], y2s_sem, y2r_sem.at[d, half],
            device_id=at_y(1 - half), device_id_type=MESH)

    def z_send(d, dz):
        return pltpu.make_async_remote_copy(
            zsend.at[d, lax.rem(z + dz, 8)], zbuf.at[d, dz - 1], zs_sem, zr_sem.at[d],
            device_id=at_z(dz), device_id_type=MESH)

    def drain(ref, sem):
        pltpu.make_async_copy(ref, ref, sem).wait()

    def x_send(d):
        return pltpu.make_async_remote_copy(
            xsend.at[d], xbuf.at[d - 1], xs_sem, xr_sem,
            device_id=at_x(4 - d), device_id_type=MESH)

    def y1_start(d):
        for slot in (1, 0):
            for half in (0, 1):
                y1_send(d, half, slot).start()

    def y2_start(d):
        for half in (0, 1):
            y1_send(d, half, 1).wait_recv()
            ysend[d, half] = part[d, half, y_rows(across(1 - half, y))] + ybuf1[d, half, 1]
            y2_send(d, half).start()

    low = lax.broadcasted_iota(jnp.int32, (8, 512), 0) < 4

    def z_start(d):
        for half in (0, 1):
            y1_send(d, half, 0).wait_recv()
            y2_send(d, half).wait_recv()
        base = pl.multiple_of(32 * y, 32)
        for u in range(4):
            left, right = [
                part[d, half, pl.ds(base + 8 * u, 8)]
                + (ybuf1[d, half, 0, 8 * u:8 * u + 8] + ybuf2[d, half, 8 * u:8 * u + 8])
                for half in (0, 1)
            ]
            zsend[d, 2 * u] = jnp.where(low, left, pltpu.roll(right, 4, 0))
            zsend[d, 2 * u + 1] = jnp.where(low, pltpu.roll(left, 4, 0), right)
        for dz in (4, 3, 5, 2, 6, 1, 7):
            z_send(d, dz).start()

    def z_end(d):
        drain(zbuf.at[d], zr_sem.at[d])
        total = zsend[d, z]
        for dz in range(1, 8):
            total = total + zbuf[d, dz - 1]
        xsend[d] = total
        if d:
            x_send(d).start()

    def own(g, carry):
        pack_one(g, 0)
        i_local(g).wait()
        i_remote(g).wait_recv()
        if q != 5:
            squeeze(g)
        multiply(g, [(0, pack.at[0, g])])
        return carry

    def far(g, carry):
        pack_one(g, 2)
        a_send(g, 2).start()
        return carry

    def near_product(g, carry):
        for d in (1, 3):
            a_send(g, d).wait_recv()
        multiply(g, [(1, recv.at[0, g]), (3, recv.at[2, g])])
        return carry

    def far_end():
        last = n_groups - 1
        a_send(last, 2).wait_recv()
        left = jnp.concatenate([recv[1, last, t] for t in range(q)], axis=1)
        for half in (0, 1):
            right = held_i[4 * last:4 * last + 4, :, 512 * half:512 * half + 512]
            right = right.reshape(4 * HALF * q, 512)
            part[2, half] += jnp.dot(left, right, preferred_element_type=F32)
            for slot in (1, 0):
                y1_send(2, half, slot).start()

    def far_product(g, carry):
        a_send(g, 2).wait_recv()
        multiply(g, [(2, recv.at[1, g])])
        return carry

    run = {
        "own": lambda: lax.fori_loop(0, n_groups, own, 0),
        "far": lambda: lax.fori_loop(0, n_groups, far, 0),
        "near_product": lambda: lax.fori_loop(0, n_groups, near_product, 0),
        "far_product": lambda: lax.fori_loop(0, n_groups - 1, far_product, 0),
        "far_end": far_end,
        "y1": y1_start, "y2": y2_start, "z": z_start, "x": z_end,
    }
    for name, *group in ORDER[q]:
        run[name](*group)
    drain(xbuf, xr_sem)
    o_ref[...] = (xsend[0] + xbuf[0]) + (xbuf[1] + xbuf[2])
    drain(i_v.at[:, pl.ds(0, 80)], is_sem)
    drain(recv, as_sem)
    drain(ybuf1, y1s_sem)
    drain(ybuf2, y2s_sem)
    drain(zbuf, zs_sem)
    drain(xbuf, xs_sem)


def ladder_call(q, amps, ints, block_map):
    n_c, n_ij, n_d = amps.shape
    n_g = n_c // 4
    dma = pltpu.SemaphoreType.DMA
    return pl.pallas_call(
        functools.partial(kernel, q),
        out_shape=jax.ShapeDtypeStruct((8, 512), F32),
        in_specs=[
            pl.BlockSpec(memory_space=pl.ANY),
            pl.BlockSpec(memory_space=pl.ANY),
            pl.BlockSpec(memory_space=pltpu.SMEM),
        ],
        out_specs=pl.BlockSpec(memory_space=pltpu.VMEM),
        scratch_shapes=[
            pltpu.VMEM((n_c, n_ij, n_d), BF16),
            pltpu.VMEM((n_c, 160, 1024), BF16),
            pltpu.VMEM((n_c if q != 5 else 1, HALF * q, 1024), BF16),
            pltpu.VMEM((4, n_g, q, 128, 128), BF16),
            pltpu.VMEM((3, n_g, q, 128, 128), BF16),
            pltpu.VMEM((2, 4, 256 * sum(map(len, tile_parts(q))), 128), BF16),
            pltpu.VMEM((4, 2, 128, 512), F32),
            pltpu.VMEM((4, 2, 2, 32, 512), F32),
            pltpu.VMEM((4, 2, 32, 512), F32),
            pltpu.VMEM((4, 2, 32, 512), F32),
            pltpu.VMEM((4, 8, 8, 512), F32),
            pltpu.VMEM((4, 7, 8, 512), F32),
            pltpu.VMEM((4, 8, 512), F32),
            pltpu.VMEM((3, 8, 512), F32),
            dma((n_g,)), dma((n_g,)), dma, dma((n_g,)),
            dma, dma((3, n_g)),
            dma, dma((4, 2, 2)),
            dma, dma((4, 2)),
            dma, dma((4,)),
            dma, dma,
        ],
        compiler_params=pltpu.CompilerParams(
            collective_id=q, has_side_effects=True, vmem_limit_bytes=56 * 2**20),
    )(amps, ints, block_map)


def on_device(amplitudes, integrals, block_map, driver):
    amps = jnp.transpose(amplitudes, (1, 0, 2))
    shares = jnp.repeat(block_map, 2, axis=1).reshape(block_map.shape[0], 4, 5).sum(axis=2)
    need = jnp.clip(jnp.max(shares), 2, 5)
    summed = lax.switch(
        need - 2, [functools.partial(ladder_call, q) for q in (2, 3, 4, 5)], amps, integrals, block_map)
    ladder = jnp.concatenate([summed[:4], summed[4:]], axis=1)
    return driver.astype(F32) + ladder


def solution(mesh):
    placed = (P("pair", "slab", None), P("slab", "pair", None), P(), P(("pair", "slab"), None))
    return jax.shard_map(
        on_device, mesh=mesh, in_specs=placed, out_specs=P(("pair", "slab"), None), check_vma=False
    )
```
